32 devices in a mesh: dp: 8 (over z, y), fsdp: 4 (over x, core).
Axes of the slice: x: 2, y: 2, z: 4, core: 2. Of those that a mesh axis runs over, the one named last changes fastest.
Arguments:
- tokens: bfloat16 [32768, 1024], P(('dp', 'fsdp')), may hold values from -6 to 6
- lengths: int32 [32, 4], P(('dp', 'fsdp')), may hold values from 0 to 512, as said below
- cotangent: bfloat16 [32768, 1024], P(('dp', 'fsdp')), may hold values from -6 to 6
- query_weight: bfloat16 [1024, 1024], P(('dp', 'fsdp')), may hold values from -0.1875 to 0.1875
- key_weight: bfloat16 [1024, 1024], P(('dp', 'fsdp')), may hold values from -0.1875 to 0.1875
- value_weight: bfloat16 [1024, 1024], P(('dp', 'fsdp')), may hold values from -0.1875 to 0.1875
- mixer_weight: bfloat16 [1024, 1024], P(('dp', 'fsdp')), may hold values from -1.5 to 1.5
- query_bias: bfloat16 [1024], P(('dp', 'fsdp')), may hold values from -3 to 3
- value_bias: bfloat16 [1024], P(('dp', 'fsdp')), may hold values from -3 to 3
- mixer_bias: bfloat16 [1024], P(('dp', 'fsdp')), may hold values from -3 to 3
- attn_gain: bfloat16 [1024], P(('dp', 'fsdp')), may hold values from 0.099609375 to 1.8984375
- attn_shift: bfloat16 [1024], P(('dp', 'fsdp')), may hold values from -3 to 3
- inner_weight: bfloat16 [1024, 4096], P(('dp', 'fsdp')), may hold values from -0.1875 to 0.1875
- inner_bias: bfloat16 [4096], P(('dp', 'fsdp')), may hold values from -3 to 3
- outer_weight: bfloat16 [4096, 1024], P(('dp', 'fsdp')), may hold values from -0.125 to 0.125
- outer_bias: bfloat16 [1024], P(('dp', 'fsdp')), may hold values from -3 to 3
- final_gain: bfloat16 [1024], P(('dp', 'fsdp')), may hold values from 0.099609375 to 1.8984375
- final_shift: bfloat16 [1024], P(('dp', 'fsdp')), may hold values from -3 to 3
Outputs:
- layer_out: bfloat16 [32768, 1024], P(('dp', 'fsdp'))
- tokens_grad: float32 [32768, 1024], P(('dp', 'fsdp'))
- query_weight_grad: float32 [1024, 1024], P(('dp', 'fsdp'))
- key_weight_grad: float32 [1024, 1024], P(('dp', 'fsdp'))
- value_weight_grad: float32 [1024, 1024], P(('dp', 'fsdp'))
- mixer_weight_grad: float32 [1024, 1024], P(('dp', 'fsdp'))
- query_bias_grad: float32 [1024], P(('dp', 'fsdp'))
- value_bias_grad: float32 [1024], P(('dp', 'fsdp'))
- mixer_bias_grad: float32 [1024], P(('dp', 'fsdp'))
- attn_gain_grad: float32 [1024], P(('dp', 'fsdp'))
- attn_shift_grad: float32 [1024], P(('dp', 'fsdp'))
- inner_weight_grad: float32 [1024, 4096], P(('dp', 'fsdp'))
- inner_bias_grad: float32 [4096], P(('dp', 'fsdp'))
- outer_weight_grad: float32 [4096, 1024], P(('dp', 'fsdp'))
- outer_bias_grad: float32 [1024], P(('dp', 'fsdp'))
- final_gain_grad: float32 [1024], P(('dp', 'fsdp'))
- final_shift_grad: float32 [1024], P(('dp', 'fsdp'))
The draws below stay inside these ranges and needn't reach their ends.
Inputs may be any that keep to these rules, and one draw needn't show every extreme that they name: Each device's lengths sum to at most 1024; its first length is 128 or more; a zero length is followed only by zeros; some device holds a sequence of exactly 512.
All inputs are finite; a program needn't handle non-finite values.
Results may differ from the reference program's by a relative error of at most 0.014.
Values may be sent and summed in bfloat16 or wider, within the bound.
A program may use at most 256 MiB of HBM per device.

```python
from functools import partial
import jax
import jax.numpy as jnp
from jax import lax

D = 1024
HEADS = 16
HEAD_DIM = 64
FF = 4096
MAXLEN = 512
SLOTS = 1024
SEQ_DEV = 4
TOKENS = 32768
DEVICES = 32


def draw_lengths(key, part):
    key = jax.random.fold_in(key, 11)
    sizes = jax.random.randint(key, (DEVICES, SEQ_DEV), MAXLEN // 4, MAXLEN + 1)
    sizes = sizes.at[0, 0].set(MAXLEN)
    bounds = jnp.cumsum(sizes, axis=1)
    return jnp.where(bounds <= SLOTS, sizes, 0).astype(jnp.int32)


def level_of(key, dims, split, least, top_value):
    gain, own = 1.0, jax.random.fold_in(key, 6)
    for axis_at, parts in split:
        steps = jnp.exp(jax.random.uniform(jax.random.fold_in(own, axis_at), (parts,), jnp.float32, least / len(split), top_value / len(split)))
        gain = gain * jnp.repeat(steps, dims[axis_at] // parts).reshape([-1 if axis == axis_at else 1 for axis in range(len(dims))])
    return gain


def noise(stream_key, dims, width, limit, split=(), kind=jnp.bfloat16):
    loudness = level_of(stream_key, dims, split, -0.22, 0.18) if split else 1.0
    entries = jax.random.normal(stream_key, dims, jnp.float32) * width * loudness
    return jnp.minimum(jnp.maximum(entries, -limit), limit).astype(kind)


def setup_inputs(seed: int = 0) -> dict:
    key_list = jax.random.split(jax.random.key(seed), 19)
    return {
        "tokens": noise(key_list[0], (TOKENS, D), 1.0, 6.0, ((0, 32),)),
        "lengths": draw_lengths(jax.random.fold_in(key_list[18], 71), 0),
        "cotangent": noise(key_list[2], (TOKENS, D), 1.0, 6.0, ((0, 32),)),
        "query_weight": noise(key_list[3], (D, D), D ** -0.5, 0.1875, ((0, 32),)),
        "key_weight": noise(key_list[4], (D, D), D ** -0.5, 0.1875, ((0, 32),)),
        "value_weight": noise(key_list[5], (D, D), D ** -0.5, 0.1875, ((0, 32),)),
        "mixer_weight": noise(key_list[6], (D, D), (D // 64) ** -0.5, 1.5, ((0, 32),)),
        "query_bias": noise(key_list[7], (D,), 0.5, 3.0, ((0, 32),)),
        "value_bias": noise(key_list[8], (D,), 0.5, 3.0, ((0, 32),)),
        "mixer_bias": noise(key_list[9], (D,), 0.5, 3.0, ((0, 32),)),
        "attn_gain": jnp.clip(1.0 + 0.18 * jax.random.normal(key_list[10], (D,), jnp.float32), 0.099609375, 1.8984375).astype(jnp.bfloat16),
        "attn_shift": noise(key_list[11], (D,), 0.5, 3.0, ((0, 32),)),
        "inner_weight": noise(key_list[12], (D, FF), D ** -0.5, 0.1875, ((0, 32),)),
        "inner_bias": noise(key_list[13], (FF,), 0.5, 3.0, ((0, 32),)),
        "outer_weight": noise(key_list[14], (FF, D), (FF // 2) ** -0.5, 0.125, ((0, 32),)),
        "outer_bias": noise(key_list[15], (D,), 0.5, 3.0, ((0, 32),)),
        "final_gain": jnp.clip(1.0 + 0.18 * jax.random.normal(key_list[16], (D,), jnp.float32), 0.099609375, 1.8984375).astype(jnp.bfloat16),
        "final_shift": noise(key_list[17], (D,), 0.5, 3.0, ((0, 32),)),
    }


EPS = 1e-06
NEG = -1e+30
HIGH = lax.Precision.HIGHEST

@jax.custom_vjp
def low(v):
    return lax.optimization_barrier(v.astype(jnp.bfloat16)).astype(jnp.float32)

@jax.custom_vjp
def low_back(v):
    return v

def low_keep(v):
    return (low(v), None)

def low_pass(kept, grad):
    return (grad,)

def back_keep(v):
    return (v, None)

def back_low(kept, grad):
    return (low(grad),)
low.defvjp(low_keep, low_pass)
low_back.defvjp(back_keep, back_low)

def slot_layout(lengths, num_rows):
    bounds = jnp.cumsum(lengths, axis=-1).astype(jnp.int32)
    position = jnp.arange(num_rows, dtype=jnp.int32)
    segment = lax.optimization_barrier(jnp.sum((position[:, None] >= bounds[..., None, :]).astype(jnp.int32), axis=-1)).astype(jnp.int32)
    usable = position < bounds[..., -1:]
    return (segment, usable)

def layer_norm(values_in, gain_vec, shift_vec):
    average = lax.optimization_barrier(jnp.mean(values_in, axis=-1, keepdims=True))
    centred = values_in - average
    spread = lax.optimization_barrier(jnp.mean(centred * centred, axis=-1, keepdims=True))
    return centred * lax.rsqrt(spread + EPS) * gain_vec + shift_vec

def product(left, right):
    return jnp.dot(left, right, precision=HIGH)

def attend(pieces):
    queries, key_rows, value_rows, segment, usable = pieces
    num_rows = queries.shape[0]
    scaled = jnp.einsum('qhd,khd->hqk', queries, key_rows, precision=HIGH) * HEAD_DIM ** (-0.5)
    position = jnp.arange(num_rows, dtype=jnp.int32)
    allowed = (segment[:, None] == segment[None, :]) & usable[None, :] | (position[:, None] == position[None, :])
    scores = low_back(jnp.where(allowed[None], scaled, NEG))
    weights = low(jax.nn.softmax(scores, axis=-1))
    return low(low_back(jnp.einsum('hqk,khd->qhd', weights, value_rows, precision=HIGH)))

def forward(segment, usable, inputs, query_weight, key_weight, value_weight, mixer_weight, query_bias, value_bias, mixer_bias, attn_gain, attn_shift, inner_weight, inner_bias, outer_weight, outer_bias, final_gain, final_shift):
    queries = low(low_back(product(inputs, query_weight) + query_bias))
    key_rows = low(low_back(product(inputs, key_weight)))
    value_rows = low(low_back(product(inputs, value_weight) + value_bias))
    shaped = (DEVICES, SLOTS, HEADS, HEAD_DIM)
    attended = lax.map(jax.checkpoint(attend), (queries.reshape(shaped), key_rows.reshape(shaped), value_rows.reshape(shaped), segment, usable))
    attended = attended.reshape(DEVICES * SLOTS, HEADS * HEAD_DIM)
    mixed = low_back(product(attended, mixer_weight) + mixer_bias)
    hidden = layer_norm(inputs + mixed, attn_gain, attn_shift)
    inner = low_back(product(low(hidden), inner_weight) + inner_bias)
    activated = low(jax.nn.gelu(inner, approximate=False))
    outer = low_back(product(activated, outer_weight) + outer_bias)
    return layer_norm(hidden + outer, final_gain, final_shift)

def reference(tokens, lengths, cotangent, query_weight, key_weight, value_weight, mixer_weight, query_bias, value_bias, mixer_bias, attn_gain, attn_shift, inner_weight, inner_bias, outer_weight, outer_bias, final_gain, final_shift):
    segment, usable = slot_layout(lengths, SLOTS)
    floats = [array_in.astype(jnp.float32) for array_in in (tokens, query_weight, key_weight, value_weight, mixer_weight, query_bias, value_bias, mixer_bias, attn_gain, attn_shift, inner_weight, inner_bias, outer_weight, outer_bias, final_gain, final_shift)]
    result, pullback = jax.vjp(partial(forward, segment, usable), *floats)
    grad_rows = cotangent.astype(jnp.float32) * usable.reshape(-1, 1).astype(jnp.float32)
    grads = pullback(grad_rows)
    return (result.astype(jnp.bfloat16), grads[0], grads[1], grads[2], grads[3], grads[4], grads[5], grads[6], grads[7], grads[8], grads[9], grads[10], grads[11], grads[12], grads[13], grads[14], grads[15])
```

```python
import jax
import jax.numpy as jnp
from jax import lax
from jax.experimental import pallas as pl
from jax.experimental.pallas import tpu as pltpu
from jax.sharding import PartitionSpec as P

HEAD_DIM = 64


EPS = 1e-06
NEG = -1e30


def slot_layout(lengths, num_rows):
    bounds = jnp.cumsum(lengths, axis=-1)
    position = jnp.arange(num_rows, dtype=jnp.int32)
    segment = jnp.sum((position[:, None] >= bounds[..., None, :]).astype(jnp.int32), axis=-1)
    usable = position < bounds[..., -1:]
    return (segment, usable)


def norm_forward(values_in, gain_vec, shift_vec):
    average = jnp.mean(values_in, axis=-1, keepdims=True)
    centred = values_in - average
    inv_std = lax.rsqrt(jnp.mean(centred * centred, axis=-1, keepdims=True) + EPS)
    normed = centred * inv_std
    return (normed * gain_vec.astype(jnp.float32) + shift_vec.astype(jnp.float32), normed, inv_std)


def norm_back(incoming, normed, inv_std, gain_vec):
    scaled = incoming * gain_vec.astype(jnp.float32)
    first_mean = jnp.mean(scaled, axis=-1, keepdims=True)
    second_mean = jnp.mean(scaled * normed, axis=-1, keepdims=True)
    values_grad = inv_std * (scaled - first_mean - normed * second_mean)
    return (values_grad, jnp.sum(incoming * normed, axis=0), jnp.sum(incoming, axis=0))


def gelu_slope(inner):
    return 0.5 * (1.0 + lax.erf(inner * 2.0 ** (-0.5))) + inner * jnp.exp(-0.5 * inner * inner) * (
        2.0 * jnp.pi
    ) ** (-0.5)


def dot_last(left, right):
    return lax.dot_general(left, right, (((1,), (1,)), ((), ())), preferred_element_type=jnp.float32)


def dot_first(left, right):
    return lax.dot_general(left, right, (((0,), (0,)), ((), ())), preferred_element_type=jnp.float32)


def attend_kernel(low_ref, high_ref, q_ref, k_ref, v_ref, idcol_ref, idrow_ref, o_ref, lse_ref):
    block = q_ref.shape[0]
    at = pl.program_id(1)
    f32 = jnp.float32
    scale = HEAD_DIM ** (-0.5)
    lane_key = lax.broadcasted_iota(jnp.int32, (block, 2 * HEAD_DIM), 1)
    first_head = lane_key < HEAD_DIM
    queries = (q_ref[...].astype(f32) * scale).astype(jnp.bfloat16)
    row_id = idcol_ref[...][:, :1]

    def step(kb, carry):
        place = pl.ds(pl.multiple_of(kb * block, block), block)
        keys = k_ref[place, :]
        vals = v_ref[place, :]
        same = row_id == idrow_ref[:1, place]
        out = []
        for head in range(2):
            top, total, acc = carry[head]
            mine = first_head if head == 0 else jnp.logical_not(first_head)
            scores = dot_last(queries, jnp.where(mine, keys, jnp.zeros_like(keys)))
            scores = jnp.where(same, scores, NEG)
            new_top = jnp.maximum(top, jnp.max(scores, axis=1, keepdims=True))
            fade = jnp.exp(top - new_top)
            weights = jnp.exp(scores - new_top)
            total = fade * total + jnp.sum(weights, axis=1, keepdims=True)
            acc = fade * acc + jnp.dot(
                weights.astype(jnp.bfloat16),
                jnp.where(mine, vals, jnp.zeros_like(vals)),
                preferred_element_type=f32,
            )
            out.append((new_top, total, acc))
        return tuple(out)

    start = (
        jnp.full((block, 1), NEG, f32),
        jnp.zeros((block, 1), f32),
        jnp.zeros((block, 2 * HEAD_DIM), f32),
    )
    one, two = lax.fori_loop(low_ref[at], high_ref[at], step, (start, start))
    o_ref[...] = (one[2] / one[1] + two[2] / two[1]).astype(o_ref.dtype)
    lse = jnp.where(first_head, one[0] + jnp.log(one[1]), two[0] + jnp.log(two[1])).T
    lse_ref[0, 0:1, :] = lse[0:1]
    lse_ref[0, 1:2, :] = lse[HEAD_DIM : HEAD_DIM + 1]


def attend_back_kernel(
    low_ref, high_ref, q_ref, k_ref, v_ref, g_ref, o_ref, lse_ref, idcol_ref, idrow_ref,
    dq_ref, dk_ref, dv_ref, dq_acc, delta_ref,
):
    block = k_ref.shape[0]
    at = pl.program_id(1)
    f32 = jnp.float32
    bf16 = jnp.bfloat16
    scale = HEAD_DIM ** (-0.5)
    lane_key = lax.broadcasted_iota(jnp.int32, (block, 2 * HEAD_DIM), 1)
    first_head = lane_key < HEAD_DIM

    @pl.when(at == 0)
    def _():
        dq_acc[...] = jnp.zeros_like(dq_acc)
        both = (g_ref[...].astype(f32) * o_ref[...].astype(f32)).T
        delta_ref[0:1, :] = jnp.sum(both[:HEAD_DIM], axis=0, keepdims=True)
        delta_ref[1:2, :] = jnp.sum(both[HEAD_DIM:], axis=0, keepdims=True)

    keys = k_ref[...]
    vals = v_ref[...]
    none = jnp.zeros_like(keys)
    key_of = (jnp.where(first_head, keys, none), jnp.where(first_head, none, keys))
    val_of = (jnp.where(first_head, vals, none), jnp.where(first_head, none, vals))
    key_id = idcol_ref[...][:, :1]

    def step(qb, carry):
        place = pl.ds(pl.multiple_of(qb * block, block), block)
        queries = (q_ref[place, :].astype(f32) * scale).astype(bf16)
        grads = g_ref[place, :]
        same = key_id == idrow_ref[:1, place]
        out = []
        dq = dq_acc[place, :]
        for head in range(2):
            dk, dv = carry[head]
            scores = dot_last(key_of[head], queries)
            weights = jnp.exp(jnp.where(same, scores - lse_ref[0, head : head + 1, place], NEG))
            weight_grad = dot_last(val_of[head], grads)
            dv = dv + jnp.dot(weights.astype(bf16), grads, preferred_element_type=f32)
            score_grad = (weights * (weight_grad - delta_ref[head : head + 1, place])).astype(bf16)
            dk = dk + jnp.dot(score_grad, queries, preferred_element_type=f32)
            dq = dq + dot_first(score_grad, key_of[head])
            out.append((dk, dv))
        dq_acc[place, :] = dq
        return tuple(out)

    zero = jnp.zeros((block, 2 * HEAD_DIM), f32)
    one, two = lax.fori_loop(low_ref[at], high_ref[at], step, ((zero, zero), (zero, zero)))
    dk_ref[...] = jnp.where(first_head, one[0], two[0]).astype(bf16)
    dv_ref[...] = jnp.where(first_head, one[1], two[1]).astype(bf16)

    @pl.when(at == pl.num_programs(1) - 1)
    def _():
        dq_ref[...] = (dq_acc[...] * scale).astype(bf16)


def attention_plan(segment, usable, block):
    num_slots = segment.shape[0]
    position = jnp.arange(num_slots, dtype=jnp.int32)
    ident = jnp.where(usable, segment, num_slots + position)
    same = ident[:, None] == ident[None, :]
    num_blocks = num_slots // block
    met = jnp.any(same.reshape(num_blocks, block, num_blocks, block), axis=(1, 3))
    order = jnp.arange(num_blocks, dtype=jnp.int32)[None, :]
    first = jnp.min(jnp.where(met, order, num_blocks), axis=1)
    last = jnp.max(jnp.where(met, order + 1, 0), axis=1)
    column = jnp.broadcast_to(ident[:, None], (num_slots, 128))
    row = jnp.broadcast_to(ident[None, :], (8, num_slots))
    return first, last, column, row


def attend(plan, queries, keys, vals, block):
    num_slots, width = queries.shape
    pairs = width // (2 * HEAD_DIM)
    first, last, column, row = plan
    lanes = 2 * HEAD_DIM
    part = pl.BlockSpec((block, lanes), lambda p, b, *_: (b, p))
    full = pl.BlockSpec((num_slots, lanes), lambda p, b, *_: (0, p))
    return pl.pallas_call(
        attend_kernel,
        grid_spec=pltpu.PrefetchScalarGridSpec(
            num_scalar_prefetch=2,
            grid=(pairs, num_slots // block),
            in_specs=[
                part, full, full,
                pl.BlockSpec((block, 128), lambda p, b, *_: (b, 0)),
                pl.BlockSpec((8, num_slots), lambda p, b, *_: (0, 0)),
            ],
            out_specs=[part, pl.BlockSpec((1, 2, block), lambda p, b, *_: (p, 0, b))],
        ),
        out_shape=[
            jax.ShapeDtypeStruct((num_slots, width), jnp.bfloat16),
            jax.ShapeDtypeStruct((pairs, 2, num_slots), jnp.float32),
        ],
        compiler_params=pltpu.CompilerParams(vmem_limit_bytes=32 * 2**20),
        cost_estimate=pl.CostEstimate(
            flops=4 * num_slots * num_slots * width,
            bytes_accessed=8 * num_slots * width,
            transcendentals=num_slots * num_slots * width // HEAD_DIM,
        ),
        name="attend",
    )(first, last, queries, keys, vals, column, row)


def attend_back(plan, queries, keys, vals, grads, attended, lse, block):
    num_slots, width = queries.shape
    pairs = width // (2 * HEAD_DIM)
    first, last, column, row = plan
    lanes = 2 * HEAD_DIM
    part = pl.BlockSpec((block, lanes), lambda p, b, *_: (b, p))
    full = pl.BlockSpec((num_slots, lanes), lambda p, b, *_: (0, p))
    return pl.pallas_call(
        attend_back_kernel,
        grid_spec=pltpu.PrefetchScalarGridSpec(
            num_scalar_prefetch=2,
            grid=(pairs, num_slots // block),
            in_specs=[
                full, part, part, full, full,
                pl.BlockSpec((1, 2, num_slots), lambda p, b, *_: (p, 0, 0)),
                pl.BlockSpec((block, 128), lambda p, b, *_: (b, 0)),
                pl.BlockSpec((8, num_slots), lambda p, b, *_: (0, 0)),
            ],
            out_specs=[full, part, part],
            scratch_shapes=[
                pltpu.VMEM((num_slots, lanes), jnp.float32),
                pltpu.VMEM((8, num_slots), jnp.float32),
            ],
        ),
        out_shape=[jax.ShapeDtypeStruct((num_slots, width), jnp.bfloat16)] * 3,
        compiler_params=pltpu.CompilerParams(vmem_limit_bytes=32 * 2**20),
        cost_estimate=pl.CostEstimate(
            flops=10 * num_slots * num_slots * width,
            bytes_accessed=16 * num_slots * width,
            transcendentals=num_slots * num_slots * width // HEAD_DIM,
        ),
        name="attend_back",
    )(first, last, queries, keys, vals, grads, attended, lse, column, row)


def col_sum(array_in):
    return jnp.sum(array_in.astype(jnp.float32), axis=0)


def vec_rows(vectors, width):
    flat = jnp.concatenate([v.reshape(v.shape[0], -1) for v in vectors], axis=1)
    rows = -(-flat.shape[1] // (16 * width)) * 16
    flat = jnp.pad(flat, ((0, 0), (0, rows * width - flat.shape[1])))
    return flat.reshape(flat.shape[0], rows, width)


def pack(devices, matrices, vectors):
    width = matrices[0].shape[1]
    parts = [m.reshape(devices, -1, width) for m in matrices]
    parts.append(vec_rows([v.reshape(devices, -1) for v in vectors], width))
    return jnp.concatenate(parts, axis=1)


def unpack(packed, matrix_rows, vector_sizes):
    devices, _, width = packed.shape
    matrices, at = [], 0
    for rows in matrix_rows:
        matrices.append(packed[:, at : at + rows].reshape(devices * rows, width))
        at += rows
    flat = packed[:, at:].reshape(devices, -1)
    vectors, at = [], 0
    for size in vector_sizes:
        vectors.append(flat[:, at : at + size].reshape(-1))
        at += size
    return matrices, vectors


def gather(packed):
    return lax.all_gather(packed[0], ("dp", "fsdp"), axis=0, tiled=False)


def scatter_sum(packed):
    return lax.psum_scatter(packed, ("dp", "fsdp"), scatter_dimension=0, tiled=True)[0]


def column_parts(matrix, width):
    return [matrix[:, at : at + width] for at in range(0, matrix.shape[1], width)]


def local(
    tokens,
    lengths,
    cotangent,
    query_weight,
    key_weight,
    value_weight,
    mixer_weight,
    query_bias,
    value_bias,
    mixer_bias,
    attn_gain,
    attn_shift,
    inner_weight,
    inner_bias,
    outer_weight,
    outer_bias,
    final_gain,
    final_shift,
):
    num_slots = tokens.shape[0]
    width = tokens.shape[1]
    devices = width // query_weight.shape[0]
    block = min(256, num_slots)
    segment, usable = slot_layout(lengths, num_slots)
    segment = segment[0]
    usable = usable[0]
    f32 = jnp.float32
    bf16 = jnp.bfloat16
    rows = query_weight.shape[0]
    ff_rows = outer_weight.shape[0]
    splits = inner_weight.shape[1] // width
    attn_packed = pack(1, [query_weight, key_weight, value_weight], [query_bias, value_bias])
    rest_packed = pack(
        1,
        [mixer_weight, *column_parts(inner_weight, width), outer_weight],
        [mixer_bias, attn_gain, attn_shift, inner_bias, outer_bias, final_gain, final_shift],
    )
    attn_all, rest_packed = lax.optimization_barrier((gather(attn_packed), rest_packed))
    (query_full, key_full, value_full), (qbias_full, vbias_full) = unpack(
        attn_all, [rows] * 3, [rows] * 2
    )
    rest_mats, rest_vecs = unpack(
        gather(rest_packed),
        [rows] * (1 + splits) + [ff_rows],
        [rows] * 3 + [ff_rows] + [rows] * 3,
    )
    mixer_full, outer_full = rest_mats[0], rest_mats[-1]
    inner_full = jnp.concatenate(rest_mats[1:-1], axis=1)
    mbias_full, again_full, ashift_full, ibias_full, obias_full, fgain_full, fshift_full = rest_vecs

    queries = (
        jnp.dot(tokens, query_full, preferred_element_type=f32) + qbias_full.astype(f32)
    ).astype(bf16)
    key_rows = jnp.dot(tokens, key_full, preferred_element_type=f32).astype(bf16)
    value_rows = (
        jnp.dot(tokens, value_full, preferred_element_type=f32) + vbias_full.astype(f32)
    ).astype(bf16)
    plan = attention_plan(segment, usable, block)
    attended, lse = attend(plan, queries, key_rows, value_rows, block)
    mixed = jnp.dot(attended, mixer_full, preferred_element_type=f32) + mbias_full.astype(f32)
    hidden, first_normed, first_inv = norm_forward(
        tokens.astype(f32) + mixed, again_full, ashift_full
    )
    hidden_low = hidden.astype(bf16)
    inner = jnp.dot(hidden_low, inner_full, preferred_element_type=f32) + ibias_full.astype(f32)
    activated = (inner * (0.5 * (1.0 + lax.erf(inner * 2.0 ** (-0.5))))).astype(bf16)
    outer = jnp.dot(activated, outer_full, preferred_element_type=f32) + obias_full.astype(f32)
    final, second_normed, second_inv = norm_forward(hidden + outer, fgain_full, fshift_full)
    layer_out = final.astype(bf16)
    out_grad = cotangent.astype(f32) * usable[:, None].astype(f32)
    second_grad, fgain_grad, fshift_grad = norm_back(
        out_grad, second_normed, second_inv, fgain_full
    )
    outer_low = second_grad.astype(bf16)
    outer_wgrad = jnp.einsum("sf,sd->fd", activated, outer_low, preferred_element_type=f32)
    outer_bgrad = col_sum(outer_low)
    act_grad = jnp.einsum("sd,fd->sf", outer_low, outer_full, preferred_element_type=f32)
    inner_low = (act_grad * gelu_slope(inner)).astype(bf16)
    inner_wgrads = [
        jnp.einsum("sd,sf->df", hidden_low, part, preferred_element_type=f32).astype(bf16)
        for part in column_parts(inner_low, width)
    ]
    inner_bgrad = col_sum(inner_low)
    hidden_grad = second_grad + jnp.einsum(
        "sf,df->sd", inner_low, inner_full, preferred_element_type=f32
    )
    first_grad, again_grad, ashift_grad = norm_back(
        hidden_grad, first_normed, first_inv, again_full
    )
    mixed_low = first_grad.astype(bf16)
    mixer_wgrad = jnp.einsum("sa,sd->ad", attended, mixed_low, preferred_element_type=f32)
    mixer_bgrad = col_sum(mixed_low)
    attended_grad = jnp.einsum(
        "sd,ad->sa", mixed_low, mixer_full, preferred_element_type=f32
    ).astype(bf16)
    rest_grads = pack(
        devices,
        [mixer_wgrad.astype(bf16), *inner_wgrads, outer_wgrad.astype(bf16)],
        [
            g.astype(bf16)
            for g in (
                mixer_bgrad, again_grad, ashift_grad, inner_bgrad, outer_bgrad, fgain_grad, fshift_grad,
            )
        ],
    )
    rest_grads, attended_grad = lax.optimization_barrier((rest_grads, attended_grad))
    rest_sums = scatter_sum(rest_grads)
    queries_grad, keys_grad, values_grad = attend_back(
        plan, queries, key_rows, value_rows, attended_grad, attended, lse, block
    )
    wgrads = [
        jnp.einsum("sd,se->de", tokens, g, preferred_element_type=f32).astype(bf16)
        for g in (queries_grad, keys_grad, values_grad)
    ]
    attn_grads = pack(
        devices, wgrads, [col_sum(queries_grad).astype(bf16), col_sum(values_grad).astype(bf16)]
    )
    attn_grads, queries_grad, keys_grad, values_grad = lax.optimization_barrier(
        (attn_grads, queries_grad, keys_grad, values_grad)
    )
    attn_sums = scatter_sum(attn_grads)
    tokens_grad = first_grad + jnp.einsum(
        "se,de->sd", queries_grad, query_full, preferred_element_type=f32
    )
    tokens_grad = tokens_grad + jnp.einsum(
        "se,de->sd", keys_grad, key_full, preferred_element_type=f32
    )
    tokens_grad = tokens_grad + jnp.einsum(
        "se,de->sd", values_grad, value_full, preferred_element_type=f32
    )
    rest_mats, rest_vecs = unpack(
        rest_sums.astype(f32)[None],
        [rows] * (1 + splits) + [ff_rows],
        [rows] * 3 + [ff_rows] + [rows] * 3,
    )
    attn_mats, attn_vecs = unpack(attn_sums.astype(f32)[None], [rows] * 3, [rows] * 2)
    return (
        layer_out,
        tokens_grad,
        attn_mats[0],
        attn_mats[1],
        attn_mats[2],
        rest_mats[0],
        attn_vecs[0],
        attn_vecs[1],
        rest_vecs[0],
        rest_vecs[1],
        rest_vecs[2],
        jnp.concatenate(rest_mats[1:-1], axis=1),
        rest_vecs[3],
        rest_mats[-1],
        rest_vecs[4],
        rest_vecs[5],
        rest_vecs[6],
    )


def solution(mesh):
    return jax.shard_map(
        local,
        mesh=mesh,
        in_specs=(
            P(("dp", "fsdp"), None),
            P(("dp", "fsdp"), None),
            P(("dp", "fsdp"), None),
            P(("dp", "fsdp"), None),
            P(("dp", "fsdp"), None),
            P(("dp", "fsdp"), None),
            P(("dp", "fsdp"), None),
            P(("dp", "fsdp")),
            P(("dp", "fsdp")),
            P(("dp", "fsdp")),
            P(("dp", "fsdp")),
            P(("dp", "fsdp")),
            P(("dp", "fsdp"), None),
            P(("dp", "fsdp")),
            P(("dp", "fsdp"), None),
            P(("dp", "fsdp")),
            P(("dp", "fsdp")),
            P(("dp", "fsdp")),
        ),
        out_specs=(
            P(("dp", "fsdp"), None),
            P(("dp", "fsdp"), None),
            P(("dp", "fsdp"), None),
            P(("dp", "fsdp"), None),
            P(("dp", "fsdp"), None),
            P(("dp", "fsdp"), None),
            P(("dp", "fsdp")),
            P(("dp", "fsdp")),
            P(("dp", "fsdp")),
            P(("dp", "fsdp")),
            P(("dp", "fsdp")),
            P(("dp", "fsdp"), None),
            P(("dp", "fsdp")),
            P(("dp", "fsdp"), None),
            P(("dp", "fsdp")),
            P(("dp", "fsdp")),
            P(("dp", "fsdp")),
        ),
        check_vma=False,
    )
```
